512 devices in a mesh: dp: 128 (over x_hi, z, y), group: 4 (over x_lo, core).
Axes of the slice: x: 4 (x_hi: 2, x_lo: 2; x = x_hi * 2 + x_lo), y: 8, z: 8, core: 2. Of those that a mesh axis runs over, the one named last changes fastest.
Arguments:
- image_embeds: bfloat16 [262144, 1152], P(('group', 'dp')), parts along dimension 0, may hold values from -0.1796875 to 0.1796875
- text_embeds: bfloat16 [262144, 1152], P(('group', 'dp')), parts along dimension 0, may hold values from -0.1796875 to 0.1796875
- logit_scale: float32 [1], replicated, may hold values from 4 to 16
- logit_bias: float32 [1], replicated, may hold values from -4 to -1
Outputs:
- image_grad: bfloat16 [262144, 1152], P(('group', 'dp')), parts along dimension 0
- text_grad: bfloat16 [262144, 1152], P(('group', 'dp')), parts along dimension 0
- image_loss: float32 [262144], P(('group', 'dp')), parts along dimension 0
The draws below stay inside these ranges and needn't reach their ends.
There are 4 independent parts, one for each index of `group`. The reference program is written for one: setup_inputs(seed, part) draws one part's arguments, and reference() takes and returns one part's arrays. A program takes and returns all parts, laid end to end along the dimension named above; an argument that names none is the same for every part. Nothing has to cross between parts.
All inputs are finite; a program needn't handle non-finite values.
Results may differ from the reference program's by a relative error of at most 0.009.
Values may be sent and summed in bfloat16 or wider, within the bound.
A program may use at most 64 MiB of HBM per device.

```python
import jax
import jax.numpy as jnp
from jax import lax

D = 1152
ROWS = 512
STEPS = 4
PAIRS = 65536
N_DP = 128


def shard_levels(key, dims, split, least, largest):
    def one(dim, parts):
        draws = jax.random.uniform(jax.random.fold_in(jax.random.fold_in(key, 6), dim), (parts,), jnp.float32, least / len(split), largest / len(split))
        return jnp.repeat(jnp.exp(draws), dims[dim] // parts).reshape((-1,) + (1,) * (len(dims) - dim - 1))

    loudness = one(*split[0])
    for cut in split[1:]:
        loudness = loudness * one(*cut)
    return loudness


def centred(own_key, extent, scale, reach, pieces=(), dtype=jnp.bfloat16):
    drawn = scale * jax.random.normal(own_key, extent, jnp.float32)
    if pieces:
        drawn = drawn * shard_levels(own_key, extent, pieces, -0.22, 0.18)
    return jnp.clip(drawn, -reach, reach).astype(dtype)


def setup_inputs(seed: int = 0, part: int = 0) -> dict:
    arg_keys = jax.random.split(jax.random.key(seed), 5)
    own_keys = jax.random.split(jax.random.fold_in(arg_keys[4], part), 5)
    return {
        "image_embeds": centred(own_keys[0], (PAIRS, D), 0.03, 0.1796875, ((0, 128),)),
        "text_embeds": centred(own_keys[1], (PAIRS, D), 0.03, 0.1796875, ((0, 128),)),
        "logit_scale": jnp.clip(jax.random.uniform(arg_keys[2], (1,), jnp.float32, 4.0, 16.0), 4.0, 16.0),
        "logit_bias": jnp.clip(jax.random.uniform(arg_keys[3], (1,), jnp.float32, -4.0, -1.0), -4.0, -1.0),
    }


EPS = 1e-06

def normalize(embeds):
    widened = embeds.astype(jnp.float32)
    inverse = lax.rsqrt(lax.optimization_barrier(jnp.sum(widened * widened, axis=-1, keepdims=True)) + EPS)
    return ((widened * inverse).astype(jnp.bfloat16), inverse)

def project_back(normed, inverse, upstream):
    widened = normed.astype(jnp.float32)
    along = lax.optimization_barrier(jnp.sum(widened * upstream, axis=-1, keepdims=True))
    return ((upstream - widened * along) * inverse).astype(jnp.bfloat16)

def reference(image_embeds, text_embeds, logit_scale, logit_bias):
    img_norm, img_inv = normalize(image_embeds)
    txt_norm, txt_inv = normalize(text_embeds)
    img_blocks = lax.optimization_barrier(img_norm).astype(jnp.float32).reshape(N_DP, ROWS, D)
    txt_blocks = lax.optimization_barrier(txt_norm).astype(jnp.float32).reshape(N_DP, ROWS, D)
    scale_value = logit_scale[0]
    bias_value = logit_bias[0]
    positions = jnp.arange(ROWS)
    diagonal = (positions[:, None] == positions[None, :]).astype(jnp.float32)
    image_acc = jnp.zeros((N_DP, ROWS, D), jnp.float32)
    text_acc = jnp.zeros((N_DP, ROWS, D), jnp.float32)
    loss_acc = jnp.zeros((N_DP, ROWS), jnp.float32)
    for offset in range(STEPS):
        visible = jnp.roll(txt_blocks, offset, axis=0)
        similar = jnp.einsum('pid,pjd->pij', img_blocks, visible)
        logits = scale_value * similar + bias_value
        if offset == 0:
            labels = 2.0 * diagonal - 1.0
        else:
            labels = -jnp.ones_like(diagonal)
        loss_acc = loss_acc + lax.optimization_barrier(jnp.sum(jax.nn.softplus(-labels * logits), axis=-1))
        logit_grad = -labels * jax.nn.sigmoid(-labels * logits)
        weights = (scale_value * logit_grad).astype(jnp.bfloat16)
        weights = lax.optimization_barrier(weights).astype(jnp.float32)
        image_acc = image_acc + jnp.einsum('pij,pjd->pid', weights, visible)
        partial_grad = jnp.einsum('pij,pid->pjd', weights, img_blocks)
        text_acc = text_acc + jnp.roll(partial_grad, -offset, axis=0)
    image_grad = project_back(img_norm, img_inv, image_acc.reshape(N_DP * ROWS, D))
    text_grad = project_back(txt_norm, txt_inv, text_acc.reshape(N_DP * ROWS, D))
    image_loss = loss_acc.reshape(N_DP * ROWS) / (STEPS * ROWS)
    return (image_grad, text_grad, image_loss)
```

```python
import functools

import jax
import jax.numpy as jnp
from jax import lax
from jax.experimental import pallas as pl
from jax.experimental.pallas import tpu as pltpu
from jax.sharding import PartitionSpec as P

STEPS = 4
EPS = 1e-06
CHUNK = 128
LANES = 128
MESH = pl.DeviceIdType.MESH


def unit_rows(raw):
    widened = raw.astype(jnp.float32)
    inverse = lax.rsqrt(jnp.sum(widened * widened, axis=-1, keepdims=True) + EPS)
    return (widened * inverse).astype(jnp.bfloat16), inverse


def kernel(cycle, scale_ref, bias_ref, img_hbm, txt_hbm, igrad_ref, tgrad_ref, loss_ref,
           raw, held, inverse, total, along, losses, in_sem, send_sem, recv_sem):
    rows, width = img_hbm.shape
    chunks = rows // CHUNK
    me = lax.axis_index("dp")
    group = lax.axis_index("group")
    after = (lax.rem(me + 1, cycle), group)
    before = (lax.rem(me + cycle - 1, cycle), group)
    targets = (before, after)
    embeds = (img_hbm, txt_hbm)
    grads = (igrad_ref, tgrad_ref)

    def piece(chunk):
        return pl.ds(pl.multiple_of(chunk * CHUNK, CHUNK), CHUNK)

    def load(side, chunk):
        return pltpu.make_async_copy(
            embeds[side].at[piece(chunk)], raw.at[side, piece(chunk)], in_sem.at[side, chunk]
        )

    def hop(side, slot, chunk):
        return pltpu.make_async_remote_copy(
            src_ref=held.at[side, slot, piece(chunk)],
            dst_ref=held.at[side, slot + 1, piece(chunk)],
            send_sem=send_sem.at[side, slot, chunk],
            recv_sem=recv_sem.at[side, slot, chunk],
            device_id=targets[side],
            device_id_type=MESH,
        )

    for chunk in range(chunks):
        for side in range(2):
            load(side, chunk).start()

    barrier = pltpu.get_barrier_semaphore()
    for neighbour in targets:
        pl.semaphore_signal(barrier, inc=1, device_id=neighbour, device_id_type=MESH)

    for chunk in range(chunks):
        for side in range(2):
            load(side, chunk).wait()
            normed, scaled = unit_rows(raw[side, piece(chunk)])
            held[side, 0, piece(chunk)] = normed
            inverse[side, piece(chunk)] = jnp.broadcast_to(scaled, (CHUNK, LANES))
            if chunk == 0 and side == 0:
                pl.semaphore_wait(barrier, 2)
            hop(side, 0, chunk).start()

    scale = scale_ref[0]
    bias = bias_ref[0]
    total[...] = jnp.zeros_like(total)
    along[...] = jnp.zeros_like(along)
    losses[...] = jnp.zeros_like(losses)
    row_index = lax.broadcasted_iota(jnp.int32, (rows, CHUNK), 0)
    column_index = lax.broadcasted_iota(jnp.int32, (rows, CHUNK), 1)

    def step(index, carry):
        slot = index // chunks
        chunk = lax.rem(index, chunks)

        @pl.when(slot > 0)
        def _():
            for side in range(2):
                hop(side, slot - 1, chunk).wait_recv()

                @pl.when(slot < STEPS - 1)
                def _():
                    hop(side, slot, chunk).start()

        positive = column_index + jnp.where(slot == 0, chunk * CHUNK, -rows) == row_index
        for side in range(2):
            own = held[side, 0]
            other = held[1 - side, slot, piece(chunk)]
            similar = lax.dot_general(
                own, other, (((1,), (1,)), ((), ())), preferred_element_type=jnp.float32
            )
            logits = scale * similar + bias
            signed = jnp.where(positive, -logits, logits)
            small = jnp.exp(-jnp.abs(signed))
            share = pl.reciprocal(1.0 + small)
            sigmoid = jnp.where(signed >= 0, share, small * share)
            weights = (scale * jnp.where(positive, -sigmoid, sigmoid)).astype(jnp.bfloat16)
            if side == 0:
                series = small * (1.0 - small * (0.5 - small * (1.0 / 3.0)))
                tail = jnp.where(small < 0.0078125, series, jnp.log(1.0 + small))
                losses[...] += jnp.maximum(signed, 0.0) + tail
            along[side] += weights.astype(jnp.float32) * similar
            total[side] += jnp.dot(weights, other, preferred_element_type=jnp.float32)
        return carry

    lax.fori_loop(0, STEPS * chunks, step, 0)

    for chunk in range(chunks):
        for side in range(2):
            part = piece(chunk)
            dot_sum = jnp.sum(along[side, part], axis=-1, keepdims=True)
            widened = held[side, 0, part].astype(jnp.float32)
            grads[side][part] = (
                (total[side, part] - widened * dot_sum) * inverse[side, part, 0:1]
            ).astype(jnp.bfloat16)
    loss_ref[...] = jnp.sum(losses[...].T, axis=0, keepdims=True) * (1.0 / (STEPS * rows))

    for chunk in range(chunks):
        for side in range(2):
            for slot in range(STEPS - 1):
                hop(side, slot, chunk).wait_send()


def local(image_embeds, text_embeds, logit_scale, logit_bias):
    rows, width = image_embeds.shape
    chunks = rows // CHUNK
    dma = pltpu.SemaphoreType.DMA
    image_grad, text_grad, loss = pl.pallas_call(
        functools.partial(kernel, lax.axis_size("dp")),
        out_shape=(
            jax.ShapeDtypeStruct((rows, width), jnp.bfloat16),
            jax.ShapeDtypeStruct((rows, width), jnp.bfloat16),
            jax.ShapeDtypeStruct((1, rows), jnp.float32),
        ),
        in_specs=[
            pl.BlockSpec(memory_space=pltpu.SMEM),
            pl.BlockSpec(memory_space=pltpu.SMEM),
            pl.BlockSpec(memory_space=pltpu.HBM),
            pl.BlockSpec(memory_space=pltpu.HBM),
        ],
        out_specs=(
            pl.BlockSpec(memory_space=pltpu.VMEM),
            pl.BlockSpec(memory_space=pltpu.VMEM),
            pl.BlockSpec(memory_space=pltpu.VMEM),
        ),
        scratch_shapes=[
            pltpu.VMEM((2, rows, width), jnp.bfloat16),
            pltpu.VMEM((2, STEPS, rows, width), jnp.bfloat16),
            pltpu.VMEM((2, rows, LANES), jnp.float32),
            pltpu.VMEM((2, rows, width), jnp.float32),
            pltpu.VMEM((2, rows, CHUNK), jnp.float32),
            pltpu.VMEM((rows, CHUNK), jnp.float32),
            dma((2, chunks)),
            dma((2, STEPS - 1, chunks)),
            dma((2, STEPS - 1, chunks)),
        ],
        compiler_params=pltpu.CompilerParams(
            collective_id=0, has_side_effects=True, vmem_limit_bytes=48 * 2**20
        ),
        cost_estimate=pl.CostEstimate(
            flops=32 * rows * rows * width, bytes_accessed=8 * rows * width, transcendentals=24 * rows * rows
        ),
        name="band_loss",
    )(logit_scale, logit_bias, image_embeds, text_embeds)
    return image_grad, text_grad, loss.reshape(rows)


def solution(mesh):
    in_specs = (P(("group", "dp"), None), P(("group", "dp"), None), P(), P())
    out_specs = (P(("group", "dp"), None), P(("group", "dp"), None), P(("group", "dp")))
    return jax.shard_map(local, mesh=mesh, in_specs=in_specs, out_specs=out_specs, check_vma=False)
```

```python
import functools

import jax
import jax.numpy as jnp
from jax import lax
from jax.experimental import pallas as pl
from jax.experimental.pallas import tpu as pltpu
from jax.sharding import PartitionSpec as P

STEPS = 4
EPS = 1e-06
CHUNK = 128
LANES = 128
LINE = 8
SEATS = 64
DETOURS = (((0, 0, 64), (0, 64, 48), (1, 0, 32)), ((0, 0, 64), (0, 64, 64), (1, 0, 48)))
RELAY_STEP = (3, 2)
DETOUR_CHUNKS = tuple(1 + max(piece[0] for piece in pieces) for pieces in DETOURS)
RELAY_ROWS = 64
MESH = pl.DeviceIdType.MESH


def unit_rows(raw):
    widened = raw.astype(jnp.float32)
    inverse = lax.rsqrt(jnp.sum(widened * widened, axis=-1, keepdims=True) + EPS)
    return (widened * inverse).astype(jnp.bfloat16), inverse


def chunk_rows(chunk):
    return pl.ds(pl.multiple_of(chunk * CHUNK, CHUNK), CHUNK)


def band_kernel(cycle, scale_ref, bias_ref, img_hbm, txt_hbm, own, inverse, total, along, losses, final, final_weights,
                raw, held, relay, in_sem, send_sem, recv_sem, relay_send, relay_recv, late_sem):
    rows, width = img_hbm.shape
    chunks = rows // CHUNK
    last = chunks - 1
    me = lax.axis_index("dp")
    group = lax.axis_index("group")
    seat = lax.rem(me, SEATS)

    def device(shift):
        return (lax.rem(me + shift + cycle, cycle), group)

    targets = (device(-1), device(1))
    embeds = (img_hbm, txt_hbm)
    first, end = seat == 0, seat == SEATS - 1
    relays = len(DETOURS[0])
    text_relay = (lax.rem(seat, LINE) == LINE - 1) & (seat < relays * LINE)
    image_relay = (lax.rem(seat, LINE) == 0) & (seat >= SEATS - relays * LINE)

    second, before_end = seat == 1, seat == SEATS - 2

    def chunk_at(side, slot, place):
        if side:
            late = (first & (slot == 1)) | (second & (slot == 2))
        else:
            late = (end & (slot == 1)) | (before_end & (slot == 2))
        return lax.rem(place + jnp.where(late, DETOUR_CHUNKS[side], 0), chunks)

    def away(place):
        return (place + 1) * LINE

    def load(side, chunk):
        return pltpu.make_async_copy(
            embeds[side].at[chunk_rows(chunk)], raw.at[side, chunk_rows(chunk)], in_sem.at[side, chunk]
        )

    def remote(source, target, done, arrived, to):
        return pltpu.make_async_remote_copy(
            src_ref=source, dst_ref=target, send_sem=done, recv_sem=arrived, device_id=to, device_id_type=MESH
        )

    def hop(side, slot, chunk, part=None, first=False):
        source = max(slot - 1, 0) if isinstance(slot, int) else jnp.maximum(slot - 1, 0)
        block = own.at[side] if first else held.at[side, source]
        span = chunk_rows(chunk) if part is None else pl.ds(chunk * CHUNK + part[0], part[1])
        return remote(
            block.at[span], held.at[side, slot, span], send_sem.at[side, slot, chunk], recv_sem.at[side, slot, chunk],
            targets[side],
        )

    def to_relay(side, place):
        chunk, start, length = DETOURS[side][place]
        return remote(
            held.at[side, 0, pl.ds(chunk * CHUNK + start, length)], relay.at[pl.ds(0, length)],
            send_sem.at[side, 1, chunk], relay_recv, device(away(place) if side else -away(place)),
        )

    def from_relay(side, place):
        chunk, start, length = DETOURS[side][place]
        return remote(
            relay.at[pl.ds(0, length)], held.at[side, 1, pl.ds(chunk * CHUNK + start, length)], relay_send,
            recv_sem.at[side, 1, chunk], device(1 - away(place) if side else away(place) - 1),
        )

    def send_by_relays(side, chunk):
        sent = sum(piece[2] for piece in DETOURS[side] if piece[0] == chunk)
        if sent < CHUNK:
            hop(side, 1, chunk, (sent, CHUNK - sent)).start()
        for place, piece in enumerate(DETOURS[side]):
            if piece[0] == chunk:
                to_relay(side, place).start()

    def relay_seat(side, place):
        return seat == (away(place) - 1 if side else SEATS - away(place))

    for chunk in range(chunks):
        for side in (1, 0):
            load(side, chunk).start()

    barrier = pltpu.get_barrier_semaphore()

    def greet(shift):
        pl.semaphore_signal(barrier, inc=1, device_id=device(shift), device_id_type=MESH)

    greet(-1)

    @pl.when(jnp.logical_not(end))
    def _():
        greet(1)

    @pl.when(first)
    def _():
        for place in range(relays):
            greet(away(place) - 1)
            greet(-away(place))

    @pl.when(text_relay)
    def _():
        greet(-1 - seat)

    @pl.when(end)
    def _():
        for place in range(relays):
            greet(1 - away(place))

    one = lambda flag, count: jnp.where(flag, count, 0)
    expected = 2 - one(first, 1) + one(text_relay, 1) + one(image_relay, 2)

    @pl.when(end)
    def _():
        pl.semaphore_wait(barrier, 2 + relays)
        pl.semaphore_signal(late_sem.at[0], inc=1, device_id=device(1), device_id_type=MESH)

    for chunk in range(chunks):
        for side in (1, 0):
            load(side, chunk).wait()
            normed, scaled = unit_rows(raw[side, chunk_rows(chunk)])
            own[side, chunk_rows(chunk)] = normed
            inverse[side, chunk_rows(chunk)] = jnp.broadcast_to(scaled, (CHUNK, LANES))
            if chunk == 0 and side == 1:
                @pl.when(jnp.logical_not(end))
                def _():
                    pl.semaphore_wait(barrier, expected)

                @pl.when(image_relay)
                def _():
                    pl.semaphore_signal(late_sem.at[1], inc=1, device_id=device(SEATS - seat), device_id_type=MESH)

            if side == 0:

                @pl.when(jnp.logical_not(first))
                def _():
                    hop(0, 0, chunk, first=True).start()

            else:
                hop(1, 0, chunk, first=True).start()

    scale = scale_ref[...].reshape(1, 1)
    bias = bias_ref[...].reshape(1, 1)
    row_index = lax.broadcasted_iota(jnp.int32, (rows, CHUNK), 0)
    column_index = lax.broadcasted_iota(jnp.int32, (rows, CHUNK), 1)

    def slopes(side, other, positive):
        similar = lax.dot_general(
            own[side], other, (((1,), (1,)), ((), ())), preferred_element_type=jnp.float32
        )
        logits = scale * similar + bias
        signed = logits if positive is None else jnp.where(positive, -logits, logits)
        small = jnp.exp(-jnp.abs(signed))
        share = pl.reciprocal(1.0 + small)
        sigmoid = jnp.where(signed >= 0, share, small * share)
        slope = sigmoid if positive is None else jnp.where(positive, -sigmoid, sigmoid)
        weights = (scale * slope).astype(jnp.bfloat16)
        if side == 0:
            series = small * (1.0 - small * (0.5 - small * (1.0 / 3.0)))
            rest = jnp.where(small < 0.0078125, series, jnp.log(1.0 + small))
            losses[...] += jnp.maximum(signed, 0.0) + rest
        along[side] += weights.astype(jnp.float32) * similar
        return weights

    def pairs(side, other, positive):
        weights = slopes(side, other, positive)
        total[side] += jnp.dot(weights, other, preferred_element_type=jnp.float32)

    total[...] = jnp.zeros_like(total)
    along[...] = jnp.zeros_like(along)
    losses[...] = jnp.zeros_like(losses)

    def own_step(chunk, carry):
        positive = column_index + chunk * CHUNK == row_index
        for side in range(2):
            pairs(side, own[1 - side, chunk_rows(chunk)], positive)
        return carry

    lax.fori_loop(0, chunks, own_step, 0)

    @pl.when(first)
    def _():
        pl.semaphore_wait(late_sem.at[0], 1)
        pl.semaphore_wait(late_sem.at[1], relays)
        for chunk in range(chunks):
            hop(0, 0, chunk, first=True).start()

    def step(index, carry):
        slot = index // chunks
        taken = [chunk_at(side, slot, lax.rem(index, chunks)) for side in range(2)]
        for side in (1, 0):
            hop(side, slot, taken[side]).wait_recv()
            by_relay = (end if side else first) & (index < DETOUR_CHUNKS[side])

            @pl.when((slot < STEPS - 2) & jnp.logical_not(by_relay))
            def _():
                hop(side, slot + 1, taken[side]).start()

            for chunk in range(DETOUR_CHUNKS[side]):

                @pl.when(by_relay & (index == chunk))
                def _():
                    send_by_relays(side, chunk)

        for side in range(2):
            pairs(side, held[1 - side, slot, chunk_rows(taken[1 - side])], None)

        for side in range(2):
            for place in range(relays):

                @pl.when(relay_seat(side, place) & (index == DETOURS[side][place][0] + RELAY_STEP[side]))
                def _():
                    to_relay(side, place).wait_recv()
                    from_relay(side, place).start()

        return carry

    lax.fori_loop(0, (STEPS - 1) * chunks - 1, step, 0)

    taken = [chunk_at(side, STEPS - 2, last) for side in range(2)]
    for side in range(2):
        hop(side, STEPS - 2, taken[side]).wait_recv()
    for side in range(2):
        other = held[1 - side, STEPS - 2, chunk_rows(taken[1 - side])]
        final[side] = other
        final_weights[side] = slopes(side, other, None)

    for slot in range(STEPS - 1):
        for chunk in range(chunks):
            for side in range(2):
                hop(side, slot, chunk, first=slot == 0).wait_send()

    for side in range(2):
        for place in range(relays):

            @pl.when(relay_seat(side, place))
            def _():
                from_relay(side, place).wait_send()


def finish_kernel(own, inverse, total, along, losses, final, final_weights, igrad_hbm, tgrad_hbm, loss_hbm,
                  outs, loss, out_sem, loss_sem):
    rows, width = own.shape[1:]
    grads = (igrad_hbm, tgrad_hbm)
    loss[...] = jnp.sum(losses[...].T, axis=0, keepdims=True) * (1.0 / (STEPS * rows))
    copies = [pltpu.make_async_copy(loss, loss_hbm, loss_sem)]
    copies[0].start()
    for chunk in range(rows // CHUNK):
        for side in range(2):
            part = chunk_rows(chunk)
            dot_sum = jnp.sum(along[side, part], axis=-1, keepdims=True)
            widened = own[side, part].astype(jnp.float32)
            rest = jnp.dot(final_weights[side, part], final[side], preferred_element_type=jnp.float32)
            outs[side, part] = (
                (total[side, part] + rest - widened * dot_sum) * inverse[side, part, 0:1]
            ).astype(jnp.bfloat16)
            copy = pltpu.make_async_copy(outs.at[side, part], grads[side].at[part], out_sem.at[side, chunk])
            copy.start()
            copies.append(copy)
    for copy in copies:
        copy.wait()


def local(image_embeds, text_embeds, logit_scale, logit_bias):
    rows, width = image_embeds.shape
    chunks = rows // CHUNK
    hops = STEPS - 1
    dma = pltpu.SemaphoreType.DMA
    vmem = pl.BlockSpec(memory_space=pltpu.VMEM)
    hbm = pl.BlockSpec(memory_space=pl.ANY)
    sums = pl.pallas_call(
        functools.partial(band_kernel, lax.axis_size("dp")),
        out_shape=(
            jax.ShapeDtypeStruct((2, rows, width), jnp.bfloat16),
            jax.ShapeDtypeStruct((2, rows, LANES), jnp.float32),
            jax.ShapeDtypeStruct((2, rows, width), jnp.float32),
            jax.ShapeDtypeStruct((2, rows, CHUNK), jnp.float32),
            jax.ShapeDtypeStruct((rows, CHUNK), jnp.float32),
            jax.ShapeDtypeStruct((2, CHUNK, width), jnp.bfloat16),
            jax.ShapeDtypeStruct((2, rows, CHUNK), jnp.bfloat16),
        ),
        in_specs=[vmem, vmem, hbm, hbm],
        out_specs=(vmem,) * 7,
        scratch_shapes=[
            pltpu.VMEM((2, rows, width), jnp.bfloat16),
            pltpu.VMEM((2, hops, rows, width), jnp.bfloat16),
            pltpu.VMEM((RELAY_ROWS, width), jnp.bfloat16),
            dma((2, chunks)),
            dma((2, hops, chunks)),
            dma((2, hops, chunks)),
            dma,
            dma,
            pltpu.SemaphoreType.REGULAR((2,)),
        ],
        compiler_params=pltpu.CompilerParams(
            collective_id=0, has_side_effects=True, vmem_limit_bytes=36 * 2**20
        ),
        cost_estimate=pl.CostEstimate(
            flops=32 * rows * rows * width, bytes_accessed=8 * rows * width, transcendentals=24 * rows * rows
        ),
        name="band_sums",
    )(
        logit_scale,
        logit_bias,
        *(pltpu.with_memory_space_constraint(array, pltpu.HBM) for array in (image_embeds, text_embeds)),
    )
    image_grad, text_grad, loss = pl.pallas_call(
        finish_kernel,
        out_shape=(
            jax.ShapeDtypeStruct((rows, width), jnp.bfloat16),
            jax.ShapeDtypeStruct((rows, width), jnp.bfloat16),
            jax.ShapeDtypeStruct((1, rows), jnp.float32),
        ),
        in_specs=[vmem] * 7,
        out_specs=(hbm,) * 3,
        scratch_shapes=[
            pltpu.VMEM((2, rows, width), jnp.bfloat16),
            pltpu.VMEM((1, rows), jnp.float32),
            dma((2, chunks)),
            dma,
        ],
        compiler_params=pltpu.CompilerParams(vmem_limit_bytes=36 * 2**20),
        cost_estimate=pl.CostEstimate(flops=8 * rows * width, bytes_accessed=16 * rows * width, transcendentals=0),
        name="finish",
    )(*sums)
    return image_grad, text_grad, loss.reshape(rows)


def solution(mesh):
    in_specs = (P(("group", "dp"), None), P(("group", "dp"), None), P(), P())
    out_specs = (P(("group", "dp"), None), P(("group", "dp"), None), P(("group", "dp")))
    return jax.shard_map(local, mesh=mesh, in_specs=in_specs, out_specs=out_specs, check_vma=False)
```

```python
import functools

import jax
import jax.numpy as jnp
from jax import lax
from jax.experimental import pallas as pl
from jax.experimental.pallas import tpu as pltpu
from jax.sharding import PartitionSpec as P

STEPS = 4
EPS = 1e-06
CHUNK = 128
LANES = 128
LINE = 8
SEATS = 64
DETOURS = (((0, 0, 64), (0, 64, 48), (1, 0, 32)), ((0, 0, 64), (0, 64, 64), (1, 0, 48)))
RELAY_STEP = (3, 2)
DETOUR_CHUNKS = tuple(1 + max(piece[0] for piece in pieces) for pieces in DETOURS)
RELAY_ROWS = 64
MESH = pl.DeviceIdType.MESH


def unit_rows(raw):
    widened = raw.astype(jnp.float32)
    inverse = lax.rsqrt(jnp.sum(widened * widened, axis=-1, keepdims=True) + EPS)
    return (widened * inverse).astype(jnp.bfloat16), inverse


def chunk_rows(chunk):
    return pl.ds(pl.multiple_of(chunk * CHUNK, CHUNK), CHUNK)


def band_kernel(cycle, scale_ref, bias_ref, img_hbm, txt_hbm, own, inverse, total, along, losses, final, final_weights,
                raw, held, relay, in_sem, send_sem, recv_sem, relay_send, relay_recv, late_sem):
    rows, width = img_hbm.shape
    chunks = rows // CHUNK
    last = chunks - 1
    me = lax.axis_index("dp")
    group = lax.axis_index("group")
    seat = lax.rem(me, SEATS)

    def device(shift):
        return (lax.rem(me + shift + cycle, cycle), group)

    targets = (device(-1), device(1))
    embeds = (img_hbm, txt_hbm)
    first, end = seat == 0, seat == SEATS - 1
    relays = len(DETOURS[0])
    text_relay = (lax.rem(seat, LINE) == LINE - 1) & (seat < relays * LINE)
    image_relay = (lax.rem(seat, LINE) == 0) & (seat >= SEATS - relays * LINE)

    second, before_end = seat == 1, seat == SEATS - 2

    def chunk_at(side, slot, place):
        if side:
            late = (first & (slot == 1)) | (second & (slot == 2))
        else:
            late = (end & (slot == 1)) | (before_end & (slot == 2))
        return lax.rem(place + jnp.where(late, DETOUR_CHUNKS[side], 0), chunks)

    def away(place):
        return (place + 1) * LINE

    def load(side, chunk):
        return pltpu.make_async_copy(
            embeds[side].at[chunk_rows(chunk)], raw.at[side, chunk_rows(chunk)], in_sem.at[side, chunk]
        )

    def remote(source, target, done, arrived, to):
        return pltpu.make_async_remote_copy(
            src_ref=source, dst_ref=target, send_sem=done, recv_sem=arrived, device_id=to, device_id_type=MESH
        )

    def hop(side, slot, chunk, part=None, first=False):
        source = max(slot - 1, 0) if isinstance(slot, int) else jnp.maximum(slot - 1, 0)
        block = own.at[side] if first else held.at[side, source]
        span = chunk_rows(chunk) if part is None else pl.ds(chunk * CHUNK + part[0], part[1])
        return remote(
            block.at[span], held.at[side, slot, span], send_sem.at[side, slot, chunk], recv_sem.at[side, slot, chunk],
            targets[side],
        )

    def to_relay(side, place):
        chunk, start, length = DETOURS[side][place]
        return remote(
            held.at[side, 0, pl.ds(chunk * CHUNK + start, length)], relay.at[pl.ds(0, length)],
            send_sem.at[side, 1, chunk], relay_recv, device(away(place) if side else -away(place)),
        )

    def from_relay(side, place):
        chunk, start, length = DETOURS[side][place]
        return remote(
            relay.at[pl.ds(0, length)], held.at[side, 1, pl.ds(chunk * CHUNK + start, length)], relay_send,
            recv_sem.at[side, 1, chunk], device(1 - away(place) if side else away(place) - 1),
        )

    def send_by_relays(side, chunk):
        sent = sum(piece[2] for piece in DETOURS[side] if piece[0] == chunk)
        if sent < CHUNK:
            hop(side, 1, chunk, (sent, CHUNK - sent)).start()
        for place, piece in enumerate(DETOURS[side]):
            if piece[0] == chunk:
                to_relay(side, place).start()

    def relay_seat(side, place):
        return seat == (away(place) - 1 if side else SEATS - away(place))

    for chunk in range(chunks):
        for side in (1, 0):
            load(side, chunk).start()

    barrier = pltpu.get_barrier_semaphore()

    def greet(shift):
        pl.semaphore_signal(barrier, inc=1, device_id=device(shift), device_id_type=MESH)

    greet(-1)

    @pl.when(jnp.logical_not(end))
    def _():
        greet(1)

    @pl.when(first)
    def _():
        for place in range(relays):
            greet(away(place) - 1)
            greet(-away(place))

    @pl.when(text_relay)
    def _():
        greet(-1 - seat)

    @pl.when(end)
    def _():
        for place in range(relays):
            greet(1 - away(place))

    one = lambda flag, count: jnp.where(flag, count, 0)
    expected = 2 - one(first, 1) + one(text_relay, 1) + one(image_relay, 2)

    @pl.when(end)
    def _():
        pl.semaphore_wait(barrier, 2 + relays)
        pl.semaphore_signal(late_sem.at[0], inc=1, device_id=device(1), device_id_type=MESH)

    for chunk in range(chunks):
        for side in (1, 0):
            load(side, chunk).wait()
            normed, scaled = unit_rows(raw[side, chunk_rows(chunk)])
            own[side, chunk_rows(chunk)] = normed
            inverse[side, chunk_rows(chunk)] = jnp.broadcast_to(scaled, (CHUNK, LANES))
            if chunk == 0 and side == 1:
                @pl.when(jnp.logical_not(end))
                def _():
                    pl.semaphore_wait(barrier, expected)

                @pl.when(image_relay)
                def _():
                    pl.semaphore_signal(late_sem.at[1], inc=1, device_id=device(SEATS - seat), device_id_type=MESH)

            if side == 0:

                @pl.when(jnp.logical_not(first))
                def _():
                    hop(0, 0, chunk, first=True).start()

            else:
                hop(1, 0, chunk, first=True).start()

    scale = scale_ref[...].reshape(1, 1)
    bias = bias_ref[...].reshape(1, 1)
    row_index = lax.broadcasted_iota(jnp.int32, (rows, CHUNK), 0)
    column_index = lax.broadcasted_iota(jnp.int32, (rows, CHUNK), 1)

    def slopes(side, other, positive):
        similar = lax.dot_general(
            own[side], other, (((1,), (1,)), ((), ())), preferred_element_type=jnp.float32
        )
        logits = scale * similar + bias
        signed = logits if positive is None else jnp.where(positive, -logits, logits)
        small = jnp.exp(-jnp.abs(signed))
        share = pl.reciprocal(1.0 + small)
        sigmoid = jnp.where(signed >= 0, share, small * share)
        slope = sigmoid if positive is None else jnp.where(positive, -sigmoid, sigmoid)
        weights = (scale * slope).astype(jnp.bfloat16)
        if side == 0:
            series = small * (1.0 - small * (0.5 - small * (1.0 / 3.0)))
            rest = jnp.where(small < 0.0078125, series, jnp.log(1.0 + small))
            losses[...] += jnp.maximum(signed, 0.0) + rest
        along[side] += weights.astype(jnp.float32) * similar
        return weights

    def pairs(side, other, positive):
        weights = slopes(side, other, positive)
        total[side] += jnp.dot(weights, other, preferred_element_type=jnp.float32)

    total[...] = jnp.zeros_like(total)
    along[...] = jnp.zeros_like(along)
    losses[...] = jnp.zeros_like(losses)

    def own_step(chunk, carry):
        positive = column_index + chunk * CHUNK == row_index
        for side in range(2):
            pairs(side, own[1 - side, chunk_rows(chunk)], positive)
        return carry

    lax.fori_loop(0, chunks, own_step, 0)

    @pl.when(first)
    def _():
        pl.semaphore_wait(late_sem.at[0], 1)
        pl.semaphore_wait(late_sem.at[1], relays)
        for chunk in range(chunks):
            hop(0, 0, chunk, first=True).start()

    def step(index, carry):
        slot = index // chunks
        taken = [chunk_at(side, slot, lax.rem(index, chunks)) for side in range(2)]
        for side in (1, 0):
            hop(side, slot, taken[side]).wait_recv()
            by_relay = (end if side else first) & (index < DETOUR_CHUNKS[side])

            @pl.when((slot < STEPS - 2) & jnp.logical_not(by_relay))
            def _():
                hop(side, slot + 1, taken[side]).start()

            for chunk in range(DETOUR_CHUNKS[side]):

                @pl.when(by_relay & (index == chunk))
                def _():
                    send_by_relays(side, chunk)

        for side in range(2):
            pairs(side, held[1 - side, slot, chunk_rows(taken[1 - side])], None)

        for side in range(2):
            for place in range(relays):

                @pl.when(relay_seat(side, place) & (index == DETOURS[side][place][0] + RELAY_STEP[side]))
                def _():
                    to_relay(side, place).wait_recv()
                    from_relay(side, place).start()

        return carry

    lax.fori_loop(0, (STEPS - 1) * chunks - 1, step, 0)

    for slot in range(STEPS - 2):
        for chunk in range(chunks):
            for side in range(2):
                hop(side, slot, chunk, first=slot == 0).wait_send()

    for side in range(2):
        for place in range(relays):

            @pl.when(relay_seat(side, place))
            def _():
                from_relay(side, place).wait_send()

    taken = [chunk_at(side, STEPS - 2, last) for side in range(2)]
    for side in range(2):
        hop(side, STEPS - 2, taken[side]).wait_recv()
    for side in range(2):
        other = held[1 - side, STEPS - 2, chunk_rows(taken[1 - side])]
        final[side] = other
        final_weights[side] = slopes(side, other, None)

    for chunk in range(chunks):
        for side in range(2):
            hop(side, STEPS - 2, chunk).wait_send()


def finish_kernel(own, inverse, total, along, losses, final, final_weights, igrad_hbm, tgrad_hbm, loss_hbm,
                  outs, loss, out_sem, loss_sem):
    rows, width = own.shape[1:]
    grads = (igrad_hbm, tgrad_hbm)
    loss[...] = jnp.sum(losses[...].T, axis=0, keepdims=True) * (1.0 / (STEPS * rows))
    copies = [pltpu.make_async_copy(loss, loss_hbm, loss_sem)]
    copies[0].start()
    for chunk in range(rows // CHUNK):
        for side in range(2):
            part = chunk_rows(chunk)
            dot_sum = jnp.sum(along[side, part], axis=-1, keepdims=True)
            widened = own[side, part].astype(jnp.float32)
            rest = jnp.dot(final_weights[side, part], final[side], preferred_element_type=jnp.float32)
            outs[side, part] = (
                (total[side, part] + rest - widened * dot_sum) * inverse[side, part, 0:1]
            ).astype(jnp.bfloat16)
            copy = pltpu.make_async_copy(outs.at[side, part], grads[side].at[part], out_sem.at[side, chunk])
            copy.start()
            copies.append(copy)
    for copy in copies:
        copy.wait()


def local(image_embeds, text_embeds, logit_scale, logit_bias):
    rows, width = image_embeds.shape
    chunks = rows // CHUNK
    hops = STEPS - 1
    dma = pltpu.SemaphoreType.DMA
    vmem = pl.BlockSpec(memory_space=pltpu.VMEM)
    hbm = pl.BlockSpec(memory_space=pl.ANY)
    sums = pl.pallas_call(
        functools.partial(band_kernel, lax.axis_size("dp")),
        out_shape=(
            jax.ShapeDtypeStruct((2, rows, width), jnp.bfloat16),
            jax.ShapeDtypeStruct((2, rows, LANES), jnp.float32),
            jax.ShapeDtypeStruct((2, rows, width), jnp.float32),
            jax.ShapeDtypeStruct((2, rows, CHUNK), jnp.float32),
            jax.ShapeDtypeStruct((rows, CHUNK), jnp.float32),
            jax.ShapeDtypeStruct((2, CHUNK, width), jnp.bfloat16),
            jax.ShapeDtypeStruct((2, rows, CHUNK), jnp.bfloat16),
        ),
        in_specs=[vmem, vmem, hbm, hbm],
        out_specs=(vmem,) * 7,
        scratch_shapes=[
            pltpu.VMEM((2, rows, width), jnp.bfloat16),
            pltpu.VMEM((2, hops, rows, width), jnp.bfloat16),
            pltpu.VMEM((RELAY_ROWS, width), jnp.bfloat16),
            dma((2, chunks)),
            dma((2, hops, chunks)),
            dma((2, hops, chunks)),
            dma,
            dma,
            pltpu.SemaphoreType.REGULAR((2,)),
        ],
        compiler_params=pltpu.CompilerParams(
            collective_id=0, has_side_effects=True, vmem_limit_bytes=36 * 2**20
        ),
        cost_estimate=pl.CostEstimate(
            flops=32 * rows * rows * width, bytes_accessed=8 * rows * width, transcendentals=24 * rows * rows
        ),
        name="band_sums",
    )(
        logit_scale,
        logit_bias,
        *(pltpu.with_memory_space_constraint(array, pltpu.HBM) for array in (image_embeds, text_embeds)),
    )
    image_grad, text_grad, loss = pl.pallas_call(
        finish_kernel,
        out_shape=(
            jax.ShapeDtypeStruct((rows, width), jnp.bfloat16),
            jax.ShapeDtypeStruct((rows, width), jnp.bfloat16),
            jax.ShapeDtypeStruct((1, rows), jnp.float32),
        ),
        in_specs=[vmem] * 7,
        out_specs=(hbm,) * 3,
        scratch_shapes=[
            pltpu.VMEM((2, rows, width), jnp.bfloat16),
            pltpu.VMEM((1, rows), jnp.float32),
            dma((2, chunks)),
            dma,
        ],
        compiler_params=pltpu.CompilerParams(vmem_limit_bytes=36 * 2**20),
        cost_estimate=pl.CostEstimate(flops=8 * rows * width, bytes_accessed=16 * rows * width, transcendentals=0),
        name="finish",
    )(*sums)
    return image_grad, text_grad, loss.reshape(rows)


def solution(mesh):
    in_specs = (P(("group", "dp"), None), P(("group", "dp"), None), P(), P())
    out_specs = (P(("group", "dp"), None), P(("group", "dp"), None), P(("group", "dp")))
    return jax.shard_map(local, mesh=mesh, in_specs=in_specs, out_specs=out_specs, check_vma=False)
```
